32 devices in a mesh: dp: 16 (over z, y, core), tensor: 2 (over x).
Axes of the slice: x: 2, y: 2, z: 4, core: 2. Of those that a mesh axis runs over, the one named last changes fastest.
Arguments:
- query_states: bfloat16 [3072, 4096], P('dp', 'tensor'), may hold values from -40 to 40
- doc_states: bfloat16 [3072, 4096], P('dp', 'tensor'), may hold values from -40 to 40
- proj_weight: bfloat16 [4096, 4096], P(None, 'tensor'), may hold values from -0.09375 to 0.09375
- left_proj: bfloat16 [4096, 64], replicated, may hold values from -0.09375 to 0.09375
- right_proj: bfloat16 [4096, 64], replicated, may hold values from -5 to 5
- positives: int32 [3072], P('dp'), may hold values from 0 to 3071
Outputs:
- query_features: float32 [3072, 4096], P('dp', 'tensor')
- doc_features: float32 [3072, 4096], P('dp', 'tensor')
The draws below stay inside these ranges and needn't reach their ends.
All inputs are finite; a program needn't handle non-finite values.
Results may differ from the reference program's by a relative error of at most 0.0033.
Values may be sent and summed in bfloat16 or wider, within the bound.
A program may use at most 128 MiB of HBM per device.

```python
import jax
import jax.numpy as jnp
from jax import lax

D = 4096
K1 = 64
K2 = 64
PAIR_DEV = 192
PAIRS = 3072
DSUB = 96


def draw_both(key):
    base = jax.random.fold_in(key, 4242)
    keys = jax.random.split(base, 7)
    row_ids = jnp.arange(PAIRS, dtype=jnp.int32)
    group = row_ids % PAIR_DEV // DSUB
    ramp = group.astype(jnp.float32)[:, None]
    ramp_dir = jnp.clip(jax.random.normal(keys[6], (D,), jnp.float32), -4.0, 4.0)
    query_base = jnp.clip(jax.random.normal(keys[0], (PAIRS, D), jnp.float32), -5.0, 5.0)
    doc_base = jnp.clip(jax.random.normal(keys[1], (PAIRS, D), jnp.float32), -5.0, 5.0)
    query_base = query_base + 0.11 * ramp_dir[None, :]
    doc_base = doc_base + 0.2 * ramp * ramp_dir[None, :]
    query_scale = jnp.exp(jax.random.uniform(keys[3], (PAIRS, 1), jnp.float32, -0.7, 1.4))
    doc_scale = jnp.exp(jax.random.uniform(keys[4], (PAIRS, 1), jnp.float32, -0.7, 1.4))
    query_rows = query_base * query_scale
    doc_rows = doc_base * doc_scale
    return (jnp.clip(query_rows, -40.0, 40.0), jnp.clip(doc_rows, -40.0, 40.0))


def draw_query_states(key, part):
    return draw_both(key)[0].astype(jnp.bfloat16)


def draw_doc_states(key, part):
    return draw_both(key)[1].astype(jnp.bfloat16)


def place_ends(result, key, least, largest):
    extent = result.shape
    spot = [jax.random.randint(jax.random.fold_in(key, axis), (), 0, extent[axis]) for axis in range(len(extent))]
    result = result.at[tuple(spot)].set(least)
    longest = extent.index(max(extent))
    spot[longest] = (spot[longest] + 1) % extent[longest]
    return result.at[tuple(spot)].set(largest)


def steps_of(rng, shape, pieces, least, high):
    def one(dim, shards_of):
        draws = jax.random.uniform(jax.random.fold_in(jax.random.fold_in(rng, 6), dim), (shards_of,), jnp.float32, least / len(pieces), high / len(pieces))
        return jnp.repeat(jnp.exp(draws), shape[dim] // shards_of).reshape((-1,) + (1,) * (len(shape) - dim - 1))

    factor_of = one(*pieces[0])
    for cut in pieces[1:]:
        factor_of = factor_of * one(*cut)
    return factor_of


def normal_values(stream_key, extent, deviation, limit, cuts=(), held_as=jnp.bfloat16):
    level = steps_of(stream_key, extent, cuts, -0.22, 0.18) if cuts else 1.0
    values = jax.random.normal(stream_key, extent, jnp.float32) * deviation * level
    return jnp.minimum(jnp.maximum(values, -limit), limit).astype(held_as)


def setup_inputs(seed: int = 0) -> dict:
    seeds = jax.random.split(jax.random.key(seed), 7)
    return {
        "query_states": draw_query_states(jax.random.fold_in(seeds[6], 71), 0),
        "doc_states": draw_doc_states(jax.random.fold_in(seeds[6], 71), 0),
        "proj_weight": normal_values(seeds[2], (D, D), D ** -0.5, 0.09375, ((1, 2),)),
        "left_proj": normal_values(seeds[3], (D, K1), D ** -0.5, 0.09375),
        "right_proj": normal_values(seeds[4], (D, K2), 1.0, 5.0),
        "positives": place_ends(jax.random.randint(seeds[5], (PAIRS,), 0, PAIRS), jax.random.fold_in(seeds[5], 1), 0, PAIRS - 1).astype(jnp.int32),
    }


epsilon = 1e-06
inverse_temp = 100.0

def unit_embed(states, weight):
    raw_rows = jnp.dot(states, weight, preferred_element_type=jnp.float32)
    scale = lax.rsqrt(lax.optimization_barrier(jnp.sum(raw_rows * raw_rows, axis=1)) + epsilon)
    return ((raw_rows * scale[:, None]).astype(jnp.bfloat16), scale)

def features(states, unit, gradient, scale, left_proj, right_proj):
    unit_wide = unit.astype(jnp.float32)
    inner = lax.optimization_barrier(jnp.sum(unit_wide * gradient, axis=1))
    pulled = (gradient - unit_wide * inner[:, None]) * scale[:, None]
    right_side = jnp.dot(pulled, right_proj.astype(jnp.float32), precision=lax.Precision.HIGHEST)
    left_side = jnp.dot(states, left_proj, preferred_element_type=jnp.float32)
    return (left_side[:, :, None] * right_side[:, None, :]).reshape(states.shape[0], -1)

def reference(query_states, doc_states, proj_weight, left_proj, right_proj, positives):
    query_unit, query_scale = unit_embed(query_states, proj_weight)
    doc_unit, doc_scale = unit_embed(doc_states, proj_weight)
    scores = jnp.dot(query_unit, doc_unit.T, preferred_element_type=jnp.float32) * inverse_temp
    row_top = lax.optimization_barrier(jnp.max(scores, axis=1))
    row_sum = lax.optimization_barrier(jnp.sum(jnp.exp(scores - row_top[:, None]), axis=1))
    lse = row_top + jnp.log(row_sum)
    doc_ids = jnp.arange(PAIRS, dtype=jnp.int32)
    onehot = (positives[:, None] == doc_ids[None, :]).astype(jnp.float32)
    weights = (jnp.exp(scores - lse[:, None]) - onehot).astype(jnp.bfloat16)
    query_grad = jnp.dot(weights, doc_unit, preferred_element_type=jnp.float32) * inverse_temp
    doc_grad = jnp.dot(weights.T, query_unit, preferred_element_type=jnp.float32) * inverse_temp
    query_features = features(query_states, query_unit, query_grad, query_scale, left_proj, right_proj)
    doc_features = features(doc_states, doc_unit, doc_grad, doc_scale, left_proj, right_proj)
    return (query_features, doc_features)
```

```python
import jax
import jax.numpy as jnp
from jax import lax
from jax.sharding import PartitionSpec as P

epsilon = 1e-06
inverse_temp = 100.0
f32 = jnp.float32
bf16 = jnp.bfloat16


def outer_rows(left_side, right_side):
    return (left_side[:, :, None] * right_side[:, None, :]).reshape(left_side.shape[0], -1)


def split_hi_lo(value, axis):
    hi = value.astype(bf16)
    lo = (value - hi.astype(f32)).astype(bf16)
    return jnp.concatenate([hi, lo], axis=axis)


def halves(product, axis):
    size = product.shape[axis] // 2
    return lax.slice_in_dim(product, 0, size, axis=axis) + lax.slice_in_dim(product, size, 2 * size, axis=axis)


def gather_columns(block, count, rank):
    if count != 2:
        return lax.all_gather(block, "tensor", axis=1, tiled=True)
    other = lax.ppermute(block, "tensor", [(0, 1), (1, 0)])
    first = jnp.where(rank == 0, block, other)
    second = jnp.where(rank == 0, other, block)
    return jnp.concatenate([first, second], axis=1)


def projected(query_states, doc_states, proj_weight, left_proj):
    count = lax.axis_size("tensor")
    rank = lax.axis_index("tensor")
    rows = query_states.shape[0]
    left_share = left_proj.shape[1] // count
    full = gather_columns(jnp.concatenate([query_states, doc_states], axis=0), count, rank)
    raw = jnp.dot(full, proj_weight, preferred_element_type=f32)
    left_mine = lax.dynamic_slice_in_dim(left_proj, rank * left_share, left_share, 1)
    left = jnp.dot(full, left_mine, preferred_element_type=f32)
    scale = lax.rsqrt(lax.psum(jnp.sum(raw * raw, axis=1), "tensor") + epsilon)
    unit = (raw * scale[:, None]).astype(bf16)
    return unit, scale, left


def local(query_states, doc_states, proj_weight, left_proj, right_proj, positives):
    count = lax.axis_size("tensor")
    rank = lax.axis_index("tensor")
    dp_count = lax.axis_size("dp")
    rows = query_states.shape[0]
    share = rows // count
    unit, scale, left = projected(query_states, doc_states, proj_weight, left_proj)
    doc_local = unit[rows:]
    if count == 2:
        mine = lax.dynamic_slice_in_dim(doc_local, rank * share, share, 0)
        theirs = lax.dynamic_slice_in_dim(doc_local, (1 - rank) * share, share, 0)
        came = lax.ppermute(theirs, "tensor", [(0, 1), (1, 0)])
        first = jnp.where(rank == 0, mine, came)
        second = jnp.where(rank == 0, came, mine)
        doc_mine = jnp.concatenate([first, second], axis=1)
    else:
        doc_mine = lax.all_to_all(doc_local, "tensor", split_axis=0, concat_axis=1, tiled=True)
    doc_block = lax.all_gather(doc_mine, "dp", axis=0, tiled=True)
    query_unit = gather_columns(unit[:rows], count, rank)
    top = jnp.concatenate([query_unit, right_proj.T], axis=0)
    product = lax.dot_general(top, doc_block, (((1,), (1,)), ((), ())), preferred_element_type=f32)
    scores = product[:rows] * inverse_temp
    doc_right = product[rows:] * inverse_temp
    query_right = jnp.dot(query_unit, right_proj, preferred_element_type=f32)
    top_part = jnp.max(scores, axis=1)
    sum_part = jnp.sum(jnp.exp(scores - top_part[:, None]), axis=1)
    parts = lax.all_gather(jnp.stack([top_part, sum_part]), "tensor")
    row_top = jnp.max(parts[:, 0], axis=0)
    lse = row_top + jnp.log(jnp.sum(parts[:, 1] * jnp.exp(parts[:, 0] - row_top), axis=0))
    column = jnp.arange(dp_count * share, dtype=jnp.int32)
    doc_ids = column // share * rows + rank * share + column % share
    onehot = (positives[:, None] == doc_ids[None, :]).astype(f32)
    weights = (jnp.exp(scores - lse[:, None]) - onehot).astype(bf16)
    weighted = weights.astype(f32) * scores
    query_sum = halves(
        lax.dot_general(
            weights, split_hi_lo(doc_right, 0), (((1,), (1,)), ((), ())), preferred_element_type=f32
        ),
        1,
    )
    query_part = query_sum - jnp.sum(weighted, axis=1)[:, None] * query_right
    doc_sum = halves(
        lax.dot_general(
            split_hi_lo(query_right * inverse_temp, 1), weights, (((0,), (0,)), ((), ())),
            preferred_element_type=f32,
        ),
        0,
    )
    doc_part = doc_sum - jnp.sum(weighted, axis=0)[None, :] * (doc_right * (1.0 / inverse_temp))
    blocks = doc_part.reshape(doc_part.shape[0], dp_count, share).transpose(1, 2, 0)
    came = lax.all_to_all(blocks, "dp", split_axis=0, concat_axis=0, tiled=True)
    right_mine = jnp.sum(came, axis=0)
    right_doc = lax.all_gather(right_mine, "tensor", axis=0, tiled=True) * scale[rows:, None]
    right_query = lax.psum(query_part, "tensor") * scale[:rows, None]
    return (outer_rows(left[:rows], right_query), outer_rows(left[rows:], right_doc))


def solution(mesh):
    placed = (P("dp", "tensor"), P("dp", "tensor"), P(None, "tensor"), P(), P(), P("dp"))
    return jax.shard_map(
        local,
        mesh=mesh,
        in_specs=placed,
        out_specs=(P("dp", "tensor"), P("dp", "tensor")),
        check_vma=False,
    )
```

```python
import functools

import jax
import jax.numpy as jnp
from jax import lax
from jax.experimental import pallas as pl
from jax.experimental.pallas import tpu as pltpu
from jax.sharding import PartitionSpec as P

epsilon = 1e-06
inverse_temp = 100.0
f32 = jnp.float32
bf16 = jnp.bfloat16


def outer_rows(left_side, right_side):
    return (left_side[:, :, None] * right_side[:, None, :]).reshape(left_side.shape[0], -1)


def split_hi_lo(value, axis):
    hi = value.astype(bf16)
    lo = (value - hi.astype(f32)).astype(bf16)
    return jnp.concatenate([hi, lo], axis=axis)


def halves(product, axis):
    size = product.shape[axis] // 2
    return lax.slice_in_dim(product, 0, size, axis=axis) + lax.slice_in_dim(product, size, 2 * size, axis=axis)


def gather_columns(block, count, rank):
    if count != 2:
        return lax.all_gather(block, "tensor", axis=1, tiled=True)
    other = lax.ppermute(block, "tensor", [(0, 1), (1, 0)])
    first = jnp.where(rank == 0, block, other)
    second = jnp.where(rank == 0, other, block)
    return jnp.concatenate([first, second], axis=1)


def projected(query_states, doc_states, proj_weight, left_proj):
    count = lax.axis_size("tensor")
    rank = lax.axis_index("tensor")
    rows = query_states.shape[0]
    left_share = left_proj.shape[1] // count
    full = gather_columns(jnp.concatenate([query_states, doc_states], axis=0), count, rank)
    raw = jnp.dot(full, proj_weight, preferred_element_type=f32)
    left_mine = lax.dynamic_slice_in_dim(left_proj, rank * left_share, left_share, 1)
    left = jnp.dot(full, left_mine, preferred_element_type=f32)
    scale = lax.rsqrt(lax.psum(jnp.sum(raw * raw, axis=1), "tensor") + epsilon)
    unit = (raw * scale[:, None]).astype(bf16)
    return unit, scale, left


def local(query_states, doc_states, proj_weight, left_proj, right_proj, positives):
    count = lax.axis_size("tensor")
    rank = lax.axis_index("tensor")
    dp_count = lax.axis_size("dp")
    rows = query_states.shape[0]
    share = rows // count
    unit, scale, left = projected(query_states, doc_states, proj_weight, left_proj)
    doc_local = unit[rows:]
    if count == 2:
        mine = lax.dynamic_slice_in_dim(doc_local, rank * share, share, 0)
        theirs = lax.dynamic_slice_in_dim(doc_local, (1 - rank) * share, share, 0)
        came = lax.ppermute(theirs, "tensor", [(0, 1), (1, 0)])
        first = jnp.where(rank == 0, mine, came)
        second = jnp.where(rank == 0, came, mine)
        doc_mine = jnp.concatenate([first, second], axis=1)
    else:
        doc_mine = lax.all_to_all(doc_local, "tensor", split_axis=0, concat_axis=1, tiled=True)
    doc_block = lax.all_gather(doc_mine, "dp", axis=0, tiled=True)
    query_unit = gather_columns(unit[:rows], count, rank)
    top = jnp.concatenate([query_unit, right_proj.T], axis=0)
    product = lax.dot_general(top, doc_block, (((1,), (1,)), ((), ())), preferred_element_type=f32)
    scores = product[:rows] * inverse_temp
    doc_right = product[rows:] * inverse_temp
    query_right = jnp.dot(query_unit, right_proj, preferred_element_type=f32)
    top_part = jnp.max(scores, axis=1)
    sum_part = jnp.sum(jnp.exp(scores - top_part[:, None]), axis=1)
    parts = lax.all_gather(jnp.stack([top_part, sum_part]), "tensor")
    row_top = jnp.max(parts[:, 0], axis=0)
    lse = row_top + jnp.log(jnp.sum(parts[:, 1] * jnp.exp(parts[:, 0] - row_top), axis=0))
    column = jnp.arange(dp_count * share, dtype=jnp.int32)
    doc_ids = column // share * rows + rank * share + column % share
    onehot = (positives[:, None] == doc_ids[None, :]).astype(f32)
    weights = (jnp.exp(scores - lse[:, None]) - onehot).astype(bf16)
    weighted = weights.astype(f32) * scores
    query_sum = halves(
        lax.dot_general(
            weights, split_hi_lo(doc_right, 0), (((1,), (1,)), ((), ())), preferred_element_type=f32
        ),
        1,
    )
    query_part = query_sum - jnp.sum(weighted, axis=1)[:, None] * query_right
    doc_sum = halves(
        lax.dot_general(
            split_hi_lo(query_right * inverse_temp, 1), weights, (((0,), (0,)), ((), ())),
            preferred_element_type=f32,
        ),
        0,
    )
    doc_part = doc_sum - jnp.sum(weighted, axis=0)[None, :] * (doc_right * (1.0 / inverse_temp))
    blocks = doc_part.reshape(doc_part.shape[0], dp_count, share).transpose(1, 2, 0)
    came = lax.all_to_all(blocks, "dp", split_axis=0, concat_axis=0, tiled=True)
    right_mine = jnp.sum(came, axis=0)
    right_doc = lax.all_gather(right_mine, "tensor", axis=0, tiled=True) * scale[rows:, None]
    right_query = lax.psum(query_part, "tensor") * scale[:rows, None]
    return (outer_rows(left[:rows], right_query), outer_rows(left[rows:], right_doc))


MESH = pl.DeviceIdType.MESH


def dot_rows(a, b):
    return lax.dot_general(a, b, (((1,), (1,)), ((), ())), preferred_element_type=f32)


def dot_plain(a, b):
    return lax.dot_general(a, b, (((1,), (0,)), ((), ())), preferred_element_type=f32)


def hi_lo(value):
    hi = value.astype(bf16)
    return hi, (value - hi.astype(f32)).astype(bf16)


def ring_kernel(
    dp_count, rows, share, width,
    top_ref, doc_ref, pos_ref, query_out, doc_out,
    held, mine, out_buf, in_buf, stat_out, stat_in, qr_out, qr_in, qrt_out, qrt_in,
    sum_out, sum_in, query_send, query_in, last_in,
    right_send, left_send, ring_recv, half_recv, sib_send, sib_recv, x_send, x_recv,
    all_send, all_recv, misc_send, misc_recv, local_sem,
):
    chips = dp_count // 2
    half = chips // 2
    me = lax.axis_index("dp")
    side = lax.axis_index("tensor")
    core = me % 2
    chip = me // 2
    spot = chip // 2 + (chip % 2) * (chips - 1 - 2 * (chip // 2))

    def dp_at(step, flag):
        q = (spot + step) % chips
        upper = q // half
        where = 2 * q + upper * (2 * (chips - 1 - q) + 1 - 2 * q)
        return 2 * where + core + flag * (1 - 2 * core)

    across = (me, 1 - side)
    right = (dp_at(1, 0), side)
    left = (dp_at(chips - 1, 0), side)
    sibling = (dp_at(0, 1), side)

    def send(src, dst, send_sem, recv_sem, device):
        return pltpu.make_async_remote_copy(
            src_ref=src, dst_ref=dst, send_sem=send_sem, recv_sem=recv_sem,
            device_id=device, device_id_type=MESH,
        )

    barrier = pltpu.get_barrier_semaphore()
    pl.semaphore_signal(barrier, inc=1, device_id=across, device_id_type=MESH)

    @pl.loop(1, dp_count)
    def _(b):
        pl.semaphore_signal(
            barrier, inc=1, device_id=(dp_at(b // 2, b % 2), side), device_id_type=MESH
        )

    pl.semaphore_wait(barrier, dp_count)

    def slot(r):
        return doc_ref if r % chips == 0 else held.at[2 * (r % chips)]

    def to_right(s):
        if s < half:
            return send(slot(chips - s + 1), held.at[2 * (chips - s)], right_send.at[s],
                        ring_recv.at[chips - s], right)
        return send(slot(chips - s + 1).at[pl.ds(0, share)], held.at[2 * half, pl.ds(0, share)],
                    right_send.at[s], ring_recv.at[half], right)

    def to_left(s):
        if s < half:
            return send(slot(s - 1), held.at[2 * s], left_send.at[s], ring_recv.at[s], left)
        return send(slot(s - 1).at[pl.ds(share, share)], held.at[2 * half, pl.ds(share, share)],
                    left_send.at[s], half_recv, left)

    def to_sibling(r):
        return send(slot(r), held.at[2 * r + 1], sib_send.at[r], sib_recv.at[r], sibling)

    def swap(b):
        return send(out_buf.at[b], in_buf.at[b], x_send.at[b], x_recv.at[b], across)

    def score(b):
        top = top_ref[...]
        out_buf[b] = dot_rows(top, held[b, pl.ds((1 - side) * share, share), :])
        swap(b).start()
        mine[b] = dot_rows(top, held[b, pl.ds(side * share, share), :])

    to_right(1).start()
    to_left(1).start()
    to_sibling(0).start()
    own = pltpu.make_async_copy(doc_ref, held.at[0], local_sem)
    own.start()
    qr_out[...] = dot_rows(top_ref[pl.ds(0, rows), :], top_ref[pl.ds(rows, width), :])
    qrt_out[...] = dot_rows(top_ref[pl.ds(rows, width), :], top_ref[pl.ds(0, rows), :])
    qr_swap = send(qr_out, qr_in, misc_send.at[0], misc_recv.at[0], across)
    qrt_swap = send(qrt_out, qrt_in, misc_send.at[1], misc_recv.at[1], across)
    qr_swap.start()
    qrt_swap.start()
    own.wait()
    score(0)
    to_sibling(0).wait_recv()
    score(1)
    for s in range(1, half):
        to_right(s).wait_recv()
        to_right(s + 1).start()
        to_sibling(chips - s).start()
        to_left(s).wait_recv()
        to_left(s + 1).start()
        to_sibling(s).start()
        to_sibling(chips - s).wait_recv()
        to_sibling(s).wait_recv()

        @pl.loop(0, 4)
        def _(k):
            score(2 * (s + (k % 2) * (chips - 2 * s)) + k // 2)

    to_right(half).wait_recv()
    to_left(half).wait_recv()
    to_sibling(half).start()
    score(2 * half)
    to_sibling(half).wait_recv()
    score(2 * half + 1)
    for s in range(1, half + 1):
        to_right(s).wait_send()
        to_left(s).wait_send()
    for r in range(chips):
        to_sibling(r).wait_send()

    def add_up(b, top):
        swap(b).wait()
        total = mine[b] + in_buf[b]
        mine[b] = total
        return jnp.maximum(top, total[:rows] * inverse_temp)

    top_wide = lax.fori_loop(0, dp_count, add_up, jnp.full((rows, share), -jnp.inf, f32))
    top_mine = jnp.max(top_wide, axis=1, keepdims=True)

    def add_exp(b, total):
        return total + jnp.exp(mine[b, pl.ds(0, rows), :] * inverse_temp - top_mine)

    sum_wide = lax.fori_loop(0, dp_count, add_exp, jnp.zeros((rows, share), f32))
    sum_mine = jnp.sum(sum_wide, axis=1, keepdims=True)
    diagonal = lax.broadcasted_iota(jnp.int32, (rows, rows), 0) == lax.broadcasted_iota(
        jnp.int32, (rows, rows), 1
    )

    def as_row(col):
        return jnp.sum(jnp.where(diagonal, col, 0.0), axis=0, keepdims=True)

    def as_col(row):
        return jnp.sum(jnp.where(diagonal, row, 0.0), axis=1, keepdims=True)

    stat_out[...] = jnp.concatenate(
        [jnp.broadcast_to(as_row(top_mine), (4, rows)), jnp.broadcast_to(as_row(sum_mine), (4, rows))],
        axis=0,
    )
    stat_swap = send(stat_out, stat_in, misc_send.at[2], misc_recv.at[2], across)
    stat_swap.start()
    qr_swap.wait()
    qrt_swap.wait()
    query_right = qr_out[...] + qr_in[...]
    turned_hi, turned_lo = hi_lo((qrt_out[...] + qrt_in[...]) * inverse_temp)
    stat_swap.wait()
    stats = stat_in[...]
    top_other = as_col(stats[0:1])
    sum_other = as_col(stats[4:5])
    row_top = jnp.maximum(top_mine, top_other)
    lse = row_top + jnp.log(
        sum_mine * jnp.exp(top_mine - row_top) + sum_other * jnp.exp(top_other - row_top)
    )
    positives = pos_ref[...]

    def share_out(b):
        return send(
            sum_out.at[b], sum_in.at[2 * ((chips - b // 2) % chips) + b % 2], all_send.at[b],
            all_recv.at[2 * ((chips - b // 2) % chips) + b % 2], (dp_at(b // 2, b % 2), side),
        )

    def gradients(b, carry):
        query_sum, inner_wide = carry
        scores = mine[b, pl.ds(0, rows), :] * inverse_temp
        doc_right = mine[b, pl.ds(rows, width), :]
        ids = lax.broadcasted_iota(jnp.int32, (rows, share), 1) + (
            dp_at(b // 2, b % 2) * rows + side * share
        )
        onehot = jnp.where(positives == ids, 1.0, 0.0)
        weights = (jnp.exp(scores - lse) - onehot).astype(bf16)
        weighted = weights.astype(f32) * scores
        right_hi, right_lo = hi_lo(doc_right * inverse_temp)
        query_sum = query_sum + dot_rows(weights, right_hi) + dot_rows(weights, right_lo)
        sum_out[b] = (
            dot_plain(turned_hi, weights) + dot_plain(turned_lo, weights)
            - jnp.sum(weighted, axis=0, keepdims=True) * doc_right
        )
        return query_sum, inner_wide + weighted

    carry = (jnp.zeros((rows, width), f32), jnp.zeros((rows, share), f32))

    def step(b, carry):
        carry = gradients(b, carry)
        share_out(b).start()
        return carry

    carry = lax.fori_loop(1, dp_count, step, carry)
    query_sum, inner_wide = gradients(0, carry)
    query_send[...] = query_sum - jnp.sum(inner_wide, axis=1, keepdims=True) * query_right
    query_swap = send(query_send, query_in, misc_send.at[3], misc_recv.at[3], across)
    query_swap.start()

    @pl.loop(1, dp_count)
    def _(b):
        share_out(b).wait()

    def collect(b, total):
        return total + sum_in[b]

    doc_sum = lax.fori_loop(1, dp_count, collect, sum_out[0])
    doc_out[side] = doc_sum
    last_swap = send(doc_out.at[side], last_in, misc_send.at[4], misc_recv.at[4], across)
    last_swap.start()
    query_swap.wait()
    query_out[...] = query_send[...] + query_in[...]
    last_swap.wait()
    doc_out[1 - side] = last_in[...]


def ring_gradients(top, docs, positives, dp_count, rows, share, width):
    chips = dp_count // 2
    depth = docs.shape[1]
    dma = pltpu.SemaphoreType.DMA
    sums = pltpu.VMEM((dp_count, width, share), f32)
    parts = pltpu.VMEM((dp_count, rows + width, share), f32)
    vmem = pl.BlockSpec(memory_space=pltpu.VMEM)
    return pl.pallas_call(
        functools.partial(ring_kernel, dp_count, rows, share, width),
        out_shape=(
            jax.ShapeDtypeStruct((rows, width), f32),
            jax.ShapeDtypeStruct((2, width, share), f32),
        ),
        in_specs=[vmem] * 3,
        out_specs=(vmem, vmem),
        scratch_shapes=[
            pltpu.VMEM((dp_count, rows, depth), bf16),
            parts, parts, parts,
            pltpu.VMEM((8, rows), f32), pltpu.VMEM((8, rows), f32),
            pltpu.VMEM((rows, width), f32), pltpu.VMEM((rows, width), f32),
            pltpu.VMEM((width, rows), f32), pltpu.VMEM((width, rows), f32),
            sums, sums,
            pltpu.VMEM((rows, width), f32), pltpu.VMEM((rows, width), f32),
            pltpu.VMEM((width, share), f32),
            dma((chips,)), dma((chips,)), dma((chips,)), dma, dma((chips,)), dma((chips,)),
            dma((dp_count,)), dma((dp_count,)), dma((dp_count,)), dma((dp_count,)),
            dma((5,)), dma((5,)), dma,
        ],
        compiler_params=pltpu.CompilerParams(
            collective_id=0, has_side_effects=True, vmem_limit_bytes=44 * 2**20
        ),
    )(top, docs, positives)


def local_ring(query_states, doc_states, proj_weight, left_proj, right_proj, positives):
    rank = lax.axis_index("tensor")
    rows = query_states.shape[0]
    share = rows // 2
    depth = proj_weight.shape[1]
    unit, scale, left = projected(query_states, doc_states, proj_weight, left_proj)
    right_mine = lax.dynamic_slice_in_dim(right_proj, rank * depth, depth, 0)
    top = jnp.concatenate([unit[:rows], right_mine.T], axis=0)
    right_query, right_doc = ring_gradients(
        top, unit[rows:], positives[:, None], lax.axis_size("dp"), rows, share, right_proj.shape[1]
    )
    right_query = right_query * scale[:rows, None]
    right_doc = right_doc.transpose(0, 2, 1).reshape(rows, -1) * scale[rows:, None]
    return (outer_rows(left[:rows], right_query), outer_rows(left[rows:], right_doc))


def solution(mesh):
    ring = mesh.shape["tensor"] == 2 and mesh.shape["dp"] % 4 == 0 and mesh.shape["dp"] >= 8
    placed = (P("dp", "tensor"), P("dp", "tensor"), P(None, "tensor"), P(), P(), P("dp"))
    return jax.shard_map(
        local_ring if ring else local,
        mesh=mesh,
        in_specs=placed,
        out_specs=(P("dp", "tensor"), P("dp", "tensor")),
        check_vma=False,
    )
```

```python
import functools

import jax
import jax.numpy as jnp
from jax import lax
from jax.experimental import pallas as pl
from jax.experimental.pallas import tpu as pltpu
from jax.sharding import PartitionSpec as P

epsilon = 1e-06
inverse_temp = 100.0
f32 = jnp.float32
bf16 = jnp.bfloat16


def outer_rows(left_side, right_side):
    return (left_side[:, :, None] * right_side[:, None, :]).reshape(left_side.shape[0], -1)


def split_hi_lo(value, axis):
    hi = value.astype(bf16)
    lo = (value - hi.astype(f32)).astype(bf16)
    return jnp.concatenate([hi, lo], axis=axis)


def halves(product, axis):
    size = product.shape[axis] // 2
    return lax.slice_in_dim(product, 0, size, axis=axis) + lax.slice_in_dim(product, size, 2 * size, axis=axis)


def gather_columns(block, count, rank):
    if count != 2:
        return lax.all_gather(block, "tensor", axis=1, tiled=True)
    other = lax.ppermute(block, "tensor", [(0, 1), (1, 0)])
    first = jnp.where(rank == 0, block, other)
    second = jnp.where(rank == 0, other, block)
    return jnp.concatenate([first, second], axis=1)


def projected(query_states, doc_states, proj_weight, left_proj):
    count = lax.axis_size("tensor")
    rank = lax.axis_index("tensor")
    rows = query_states.shape[0]
    left_share = left_proj.shape[1] // count
    full = gather_columns(jnp.concatenate([query_states, doc_states], axis=0), count, rank)
    raw = jnp.dot(full, proj_weight, preferred_element_type=f32)
    left_mine = lax.dynamic_slice_in_dim(left_proj, rank * left_share, left_share, 1)
    left = jnp.dot(full, left_mine, preferred_element_type=f32)
    scale = lax.rsqrt(lax.psum(jnp.sum(raw * raw, axis=1), "tensor") + epsilon)
    unit = (raw * scale[:, None]).astype(bf16)
    return unit, scale, left


def local(query_states, doc_states, proj_weight, left_proj, right_proj, positives):
    count = lax.axis_size("tensor")
    rank = lax.axis_index("tensor")
    dp_count = lax.axis_size("dp")
    rows = query_states.shape[0]
    share = rows // count
    unit, scale, left = projected(query_states, doc_states, proj_weight, left_proj)
    doc_local = unit[rows:]
    if count == 2:
        mine = lax.dynamic_slice_in_dim(doc_local, rank * share, share, 0)
        theirs = lax.dynamic_slice_in_dim(doc_local, (1 - rank) * share, share, 0)
        came = lax.ppermute(theirs, "tensor", [(0, 1), (1, 0)])
        first = jnp.where(rank == 0, mine, came)
        second = jnp.where(rank == 0, came, mine)
        doc_mine = jnp.concatenate([first, second], axis=1)
    else:
        doc_mine = lax.all_to_all(doc_local, "tensor", split_axis=0, concat_axis=1, tiled=True)
    doc_block = lax.all_gather(doc_mine, "dp", axis=0, tiled=True)
    query_unit = gather_columns(unit[:rows], count, rank)
    top = jnp.concatenate([query_unit, right_proj.T], axis=0)
    product = lax.dot_general(top, doc_block, (((1,), (1,)), ((), ())), preferred_element_type=f32)
    scores = product[:rows] * inverse_temp
    doc_right = product[rows:] * inverse_temp
    query_right = jnp.dot(query_unit, right_proj, preferred_element_type=f32)
    top_part = jnp.max(scores, axis=1)
    sum_part = jnp.sum(jnp.exp(scores - top_part[:, None]), axis=1)
    parts = lax.all_gather(jnp.stack([top_part, sum_part]), "tensor")
    row_top = jnp.max(parts[:, 0], axis=0)
    lse = row_top + jnp.log(jnp.sum(parts[:, 1] * jnp.exp(parts[:, 0] - row_top), axis=0))
    column = jnp.arange(dp_count * share, dtype=jnp.int32)
    doc_ids = column // share * rows + rank * share + column % share
    onehot = (positives[:, None] == doc_ids[None, :]).astype(f32)
    weights = (jnp.exp(scores - lse[:, None]) - onehot).astype(bf16)
    weighted = weights.astype(f32) * scores
    query_sum = halves(
        lax.dot_general(
            weights, split_hi_lo(doc_right, 0), (((1,), (1,)), ((), ())), preferred_element_type=f32
        ),
        1,
    )
    query_part = query_sum - jnp.sum(weighted, axis=1)[:, None] * query_right
    doc_sum = halves(
        lax.dot_general(
            split_hi_lo(query_right * inverse_temp, 1), weights, (((0,), (0,)), ((), ())),
            preferred_element_type=f32,
        ),
        0,
    )
    doc_part = doc_sum - jnp.sum(weighted, axis=0)[None, :] * (doc_right * (1.0 / inverse_temp))
    blocks = doc_part.reshape(doc_part.shape[0], dp_count, share).transpose(1, 2, 0)
    came = lax.all_to_all(blocks, "dp", split_axis=0, concat_axis=0, tiled=True)
    right_mine = jnp.sum(came, axis=0)
    right_doc = lax.all_gather(right_mine, "tensor", axis=0, tiled=True) * scale[rows:, None]
    right_query = lax.psum(query_part, "tensor") * scale[:rows, None]
    return (outer_rows(left[:rows], right_query), outer_rows(left[rows:], right_doc))


MESH = pl.DeviceIdType.MESH


def dot_rows(a, b):
    return lax.dot_general(a, b, (((1,), (1,)), ((), ())), preferred_element_type=f32)


def dot_plain(a, b):
    return lax.dot_general(a, b, (((1,), (0,)), ((), ())), preferred_element_type=f32)


def hi_lo(value):
    hi = value.astype(bf16)
    return hi, (value - hi.astype(f32)).astype(bf16)


pieces = 4
tiles = 4


def ring_kernel(
    dp_count, rows, share, width,
    query_ref, doc_ref, weight_ref, left_ref, right_ref, pos_ref,
    query_out, doc_out, scale_out, left_out,
    weight, query_raw, doc_raw, query_came, doc_came, top_ref,
    held, mine, out_buf, in_buf, stat_out, stat_in, qr_out, qr_in, qrt_out, qrt_in,
    sum_out, sum_in, query_send, query_in, last_in,
    right_send, left_send, ring_recv, half_recv, sib_send, sib_recv, x_send, x_recv,
    all_send, all_recv, misc_send, misc_recv, local_sem, state_send, state_recv,
):
    depth = query_ref.shape[1]
    piece = depth // pieces
    tile = depth // tiles
    chips = dp_count // 2
    half = chips // 2
    me = lax.axis_index("dp")
    side = lax.axis_index("tensor")
    core = me % 2
    chip = me // 2
    spot = chip // 2 + (chip % 2) * (chips - 1 - 2 * (chip // 2))

    def dp_at(step, flag):
        q = (spot + step) % chips
        upper = q // half
        where = 2 * q + upper * (2 * (chips - 1 - q) + 1 - 2 * q)
        return 2 * where + core + flag * (1 - 2 * core)

    across = (me, 1 - side)
    right = (dp_at(1, 0), side)
    left = (dp_at(chips - 1, 0), side)
    sibling = (dp_at(0, 1), side)

    def send(src, dst, send_sem, recv_sem, device):
        return pltpu.make_async_remote_copy(
            src_ref=src, dst_ref=dst, send_sem=send_sem, recv_sem=recv_sem,
            device_id=device, device_id_type=MESH,
        )

    loads = [
        pltpu.make_async_copy(
            weight_ref.at[pl.ds(pl.multiple_of(which * depth, depth), depth)], weight.at[i], local_sem.at[i]
        )
        for i, which in enumerate((side, 1 - side))
    ]
    for load in loads:
        load.start()

    barrier = pltpu.get_barrier_semaphore()
    pl.semaphore_signal(barrier, inc=1, device_id=across, device_id_type=MESH)

    @pl.loop(1, dp_count)
    def _(b):
        pl.semaphore_signal(
            barrier, inc=1, device_id=(dp_at(b // 2, b % 2), side), device_id_type=MESH
        )

    pl.semaphore_wait(barrier, dp_count)

    def slot(r):
        return held.at[2 * (r % chips)]

    def to_right(s):
        if s < half:
            return send(slot(chips - s + 1), held.at[2 * (chips - s)], right_send.at[s],
                        ring_recv.at[chips - s], right)
        return send(slot(chips - s + 1).at[pl.ds(0, share)], held.at[2 * half, pl.ds(0, share)],
                    right_send.at[s], ring_recv.at[half], right)

    def to_left(s):
        if s < half:
            return send(slot(s - 1), held.at[2 * s], left_send.at[s], ring_recv.at[s], left)
        return send(slot(s - 1).at[pl.ds(share, share)], held.at[2 * half, pl.ds(share, share)],
                    left_send.at[s], half_recv, left)

    def to_sibling(r):
        return send(slot(r), held.at[2 * r + 1], sib_send.at[r], sib_recv.at[r], sibling)

    def swap(b):
        return send(out_buf.at[b], in_buf.at[b], x_send.at[b], x_recv.at[b], across)

    def score(b):
        top = top_ref[...]
        out_buf[b] = dot_rows(top, held[b, pl.ds((1 - side) * share, share), :])
        swap(b).start()
        mine[b] = dot_rows(top, held[b, pl.ds(side * share, share), :])

    diagonal = lax.broadcasted_iota(jnp.int32, (rows, rows), 0) == lax.broadcasted_iota(
        jnp.int32, (rows, rows), 1
    )

    def as_row(col):
        return jnp.sum(jnp.where(diagonal, col, 0.0), axis=0, keepdims=True)

    def as_col(row):
        return jnp.sum(jnp.where(diagonal, row, 0.0), axis=1, keepdims=True)

    def swap_piece(src, dst, k, at):
        part = pl.ds(k * piece, piece)
        return send(src.at[:, part], dst.at[:, part], state_send.at[at + k], state_recv.at[at + k], across)

    doc_pieces = [swap_piece(doc_ref, doc_came, k, 0) for k in range(pieces)]
    query_pieces = [swap_piece(query_ref, query_came, k, pieces) for k in range(pieces)]
    for copy in doc_pieces:
        copy.start()

    def left_of(which):
        return left_ref[:, pl.ds(pl.multiple_of(which * depth, depth), depth)]

    def project_mine(states, raw):
        @pl.loop(0, tiles)
        def _(n):
            cols = pl.ds(pl.multiple_of(n * tile, tile), tile)
            raw[:, cols] = dot_plain(states[...], weight[0, :, cols])

    def project_piece(states, raw, k):
        part = pl.ds(k * piece, piece)

        @pl.loop(0, tiles)
        def _(n):
            cols = pl.ds(pl.multiple_of(n * tile, tile), tile)
            raw[:, cols] += dot_plain(states[:, part], weight[1, part, cols])

    def squares(raw):
        def add(n, total):
            block = raw[:, pl.ds(pl.multiple_of(n * 128, 128), 128)]
            return total + block * block

        total = lax.fori_loop(0, depth // 128, add, jnp.zeros((rows, 128), f32))
        return jnp.sum(total, axis=1, keepdims=True)

    def stat_copy(i):
        return send(stat_out.at[i], stat_in.at[i], misc_send.at[i], misc_recv.at[i], across)

    def normalize(raw, scale, store):
        @pl.loop(0, tiles)
        def _(n):
            cols = pl.ds(pl.multiple_of(n * tile, tile), tile)
            store(cols, (raw[:, cols] * scale).astype(bf16))

    def store_doc(cols, value):
        held[0, :, cols] = value

    def store_query(cols, value):
        top_ref[pl.ds(0, rows), cols] = value

    loads[0].wait()
    project_mine(doc_ref, doc_raw)
    project_mine(query_ref, query_raw)
    left_out[pl.ds(0, rows), :] = dot_rows(query_ref[...], left_of(side))
    left_out[pl.ds(rows, rows), :] = dot_rows(doc_ref[...], left_of(side))
    loads[1].wait()
    for k in range(pieces):
        doc_pieces[k].wait_recv()
        project_piece(doc_came, doc_raw, k)
    doc_sq = as_row(squares(doc_raw))
    stat_out[0] = jnp.broadcast_to(doc_sq, (8, rows))
    stat_copy(0).start()
    for copy in query_pieces:
        copy.start()
    left_out[pl.ds(rows, rows), :] += dot_rows(doc_came[...], left_of(1 - side))
    stat_copy(0).wait()
    doc_scale = lax.rsqrt(doc_sq + stat_in[0, pl.ds(0, 1), :] + epsilon)
    scale_out[...] = jnp.broadcast_to(doc_scale, (8, rows))
    normalize(doc_raw, as_col(doc_scale), store_doc)
    to_right(1).start()
    to_left(1).start()
    to_sibling(0).start()
    top_ref[pl.ds(rows, width), :] = right_ref[...]
    for k in range(pieces):
        query_pieces[k].wait_recv()
        project_piece(query_came, query_raw, k)
    query_sq = squares(query_raw)
    stat_out[1] = jnp.broadcast_to(as_row(query_sq), (8, rows))
    stat_copy(1).start()
    left_out[pl.ds(0, rows), :] += dot_rows(query_came[...], left_of(1 - side))
    stat_copy(1).wait()
    query_scale = lax.rsqrt(query_sq + as_col(stat_in[1, pl.ds(0, 1), :]) + epsilon)
    normalize(query_raw, query_scale, store_query)
    qr_swap = send(qr_out, qr_in, misc_send.at[3], misc_recv.at[3], across)
    qrt_swap = send(qrt_out, qrt_in, misc_send.at[4], misc_recv.at[4], across)
    for s in range(1, half):
        to_right(s).wait_recv()
        to_right(s + 1).start()
        to_sibling(chips - s).start()
        to_left(s).wait_recv()
        to_left(s + 1).start()
        to_sibling(s).start()
        if s == 1:
            qr_out[...] = dot_rows(top_ref[pl.ds(0, rows), :], top_ref[pl.ds(rows, width), :])
            qrt_out[...] = dot_rows(top_ref[pl.ds(rows, width), :], top_ref[pl.ds(0, rows), :])
            qr_swap.start()
            qrt_swap.start()
            to_sibling(0).wait_recv()

            @pl.loop(0, 2)
            def _(k):
                score(k)

        to_sibling(chips - s).wait_recv()
        to_sibling(s).wait_recv()

        @pl.loop(0, 4)
        def _(k):
            score(2 * (s + (k % 2) * (chips - 2 * s)) + k // 2)

    to_right(half).wait_recv()
    to_left(half).wait_recv()
    to_sibling(half).start()
    score(2 * half)
    to_sibling(half).wait_recv()
    score(2 * half + 1)
    for s in range(1, half + 1):
        to_right(s).wait_send()
        to_left(s).wait_send()
    for r in range(chips):
        to_sibling(r).wait_send()
    for copy in doc_pieces + query_pieces:
        copy.wait_send()

    def add_up(b, top):
        swap(b).wait()
        total = mine[b] + in_buf[b]
        mine[b] = total
        return jnp.maximum(top, total[:rows] * inverse_temp)

    top_wide = lax.fori_loop(0, dp_count, add_up, jnp.full((rows, share), -jnp.inf, f32))
    top_mine = jnp.max(top_wide, axis=1, keepdims=True)

    def add_exp(b, total):
        return total + jnp.exp(mine[b, pl.ds(0, rows), :] * inverse_temp - top_mine)

    sum_wide = lax.fori_loop(0, dp_count, add_exp, jnp.zeros((rows, share), f32))
    sum_mine = jnp.sum(sum_wide, axis=1, keepdims=True)
    stat_out[2] = jnp.concatenate(
        [jnp.broadcast_to(as_row(top_mine), (4, rows)), jnp.broadcast_to(as_row(sum_mine), (4, rows))],
        axis=0,
    )
    stat_copy(2).start()
    qr_swap.wait()
    qrt_swap.wait()
    query_right = qr_out[...] + qr_in[...]
    turned_hi, turned_lo = hi_lo((qrt_out[...] + qrt_in[...]) * inverse_temp)
    stat_copy(2).wait()
    stats = stat_in[2]
    top_other = as_col(stats[0:1])
    sum_other = as_col(stats[4:5])
    row_top = jnp.maximum(top_mine, top_other)
    lse = row_top + jnp.log(
        sum_mine * jnp.exp(top_mine - row_top) + sum_other * jnp.exp(top_other - row_top)
    )
    positives = pos_ref[...]

    def share_out(b):
        return send(
            sum_out.at[b], sum_in.at[2 * ((chips - b // 2) % chips) + b % 2], all_send.at[b],
            all_recv.at[2 * ((chips - b // 2) % chips) + b % 2], (dp_at(b // 2, b % 2), side),
        )

    def gradients(b, carry):
        query_sum, inner_wide = carry
        scores = mine[b, pl.ds(0, rows), :] * inverse_temp
        doc_right = mine[b, pl.ds(rows, width), :]
        ids = lax.broadcasted_iota(jnp.int32, (rows, share), 1) + (
            dp_at(b // 2, b % 2) * rows + side * share
        )
        onehot = jnp.where(positives == ids, 1.0, 0.0)
        weights = (jnp.exp(scores - lse) - onehot).astype(bf16)
        weighted = weights.astype(f32) * scores
        right_hi, right_lo = hi_lo(doc_right * inverse_temp)
        query_sum = query_sum + dot_rows(weights, right_hi) + dot_rows(weights, right_lo)
        sum_out[b] = (
            dot_plain(turned_hi, weights) + dot_plain(turned_lo, weights)
            - jnp.sum(weighted, axis=0, keepdims=True) * doc_right
        )
        return query_sum, inner_wide + weighted

    carry = (jnp.zeros((rows, width), f32), jnp.zeros((rows, share), f32))

    def step(b, carry):
        carry = gradients(b, carry)
        share_out(b).start()
        return carry

    carry = lax.fori_loop(1, dp_count, step, carry)
    query_sum, inner_wide = gradients(0, carry)
    query_send[...] = query_sum - jnp.sum(inner_wide, axis=1, keepdims=True) * query_right
    query_swap = send(query_send, query_in, misc_send.at[5], misc_recv.at[5], across)
    query_swap.start()

    @pl.loop(1, dp_count)
    def _(b):
        share_out(b).wait()

    def collect(b, total):
        return total + sum_in[b]

    doc_sum = lax.fori_loop(1, dp_count, collect, sum_out[0])
    doc_out[side] = doc_sum
    last_swap = send(doc_out.at[side], last_in, misc_send.at[6], misc_recv.at[6], across)
    last_swap.start()
    query_swap.wait()
    query_out[...] = (query_send[...] + query_in[...]) * query_scale
    last_swap.wait()
    doc_out[1 - side] = last_in[...]


def ring_gradients(query_states, doc_states, proj_weight, left_turned, right_turned, positives, dp_count):
    chips = dp_count // 2
    rows, depth = doc_states.shape
    share = rows // 2
    width = right_turned.shape[0]
    dma = pltpu.SemaphoreType.DMA
    sums = pltpu.VMEM((dp_count, width, share), f32)
    parts = pltpu.VMEM((dp_count, rows + width, share), f32)
    vmem = pl.BlockSpec(memory_space=pltpu.VMEM)
    raw = pltpu.VMEM((rows, depth), f32)
    states = pltpu.VMEM((rows, depth), bf16)
    return pl.pallas_call(
        functools.partial(ring_kernel, dp_count, rows, share, width),
        out_shape=(
            jax.ShapeDtypeStruct((rows, width), f32),
            jax.ShapeDtypeStruct((2, width, share), f32),
            jax.ShapeDtypeStruct((8, rows), f32),
            jax.ShapeDtypeStruct((2 * rows, left_turned.shape[0]), f32),
        ),
        in_specs=[vmem, vmem, pl.BlockSpec(memory_space=pl.ANY), vmem, vmem, vmem],
        out_specs=(vmem, vmem, vmem, vmem),
        scratch_shapes=[
            pltpu.VMEM((2, depth, depth), bf16),
            raw, raw, states, states,
            pltpu.VMEM((rows + width, depth), bf16),
            pltpu.VMEM((dp_count, rows, depth), bf16),
            parts, parts, parts,
            pltpu.VMEM((3, 8, rows), f32), pltpu.VMEM((3, 8, rows), f32),
            pltpu.VMEM((rows, width), f32), pltpu.VMEM((rows, width), f32),
            pltpu.VMEM((width, rows), f32), pltpu.VMEM((width, rows), f32),
            sums, sums,
            pltpu.VMEM((rows, width), f32), pltpu.VMEM((rows, width), f32),
            pltpu.VMEM((width, share), f32),
            dma((chips,)), dma((chips,)), dma((chips,)), dma, dma((chips,)), dma((chips,)),
            dma((dp_count,)), dma((dp_count,)), dma((dp_count,)), dma((dp_count,)),
            dma((7,)), dma((7,)), dma((2,)), dma((2 * pieces,)), dma((2 * pieces,)),
        ],
        compiler_params=pltpu.CompilerParams(
            collective_id=0, has_side_effects=True, vmem_limit_bytes=57 * 2**20
        ),
    )(query_states, doc_states, proj_weight, left_turned, right_turned, positives)


def local_ring(query_states, doc_states, proj_weight, left_proj, right_proj, positives):
    rank = lax.axis_index("tensor")
    rows = query_states.shape[0]
    depth = proj_weight.shape[1]
    left_share = left_proj.shape[1] // 2
    right_mine = lax.dynamic_slice_in_dim(right_proj, rank * depth, depth, 0)
    left_mine = lax.dynamic_slice_in_dim(left_proj, rank * left_share, left_share, 1)
    right_query, right_doc, scale, left = ring_gradients(
        query_states, doc_states, proj_weight, left_mine.T, right_mine.T, positives[:, None],
        lax.axis_size("dp"),
    )
    right_doc = right_doc.transpose(0, 2, 1).reshape(rows, -1) * scale[0][:, None]
    return (outer_rows(left[:rows], right_query), outer_rows(left[rows:], right_doc))


def solution(mesh):
    ring = mesh.shape["tensor"] == 2 and mesh.shape["dp"] % 4 == 0 and mesh.shape["dp"] >= 8
    placed = (P("dp", "tensor"), P("dp", "tensor"), P(None, "tensor"), P(), P(), P("dp"))
    return jax.shard_map(
        local_ring if ring else local,
        mesh=mesh,
        in_specs=placed,
        out_specs=(P("dp", "tensor"), P("dp", "tensor")),
        check_vma=False,
    )
```

```python
import functools

import jax
import jax.numpy as jnp
from jax import lax
from jax.experimental import pallas as pl
from jax.experimental.pallas import tpu as pltpu
from jax.sharding import PartitionSpec as P

epsilon = 1e-06
inverse_temp = 100.0
f32 = jnp.float32
bf16 = jnp.bfloat16


def outer_rows(left_side, right_side):
    return (left_side[:, :, None] * right_side[:, None, :]).reshape(left_side.shape[0], -1)


def split_hi_lo(value, axis):
    hi = value.astype(bf16)
    lo = (value - hi.astype(f32)).astype(bf16)
    return jnp.concatenate([hi, lo], axis=axis)


def halves(product, axis):
    size = product.shape[axis] // 2
    return lax.slice_in_dim(product, 0, size, axis=axis) + lax.slice_in_dim(product, size, 2 * size, axis=axis)


def gather_columns(block, count, rank):
    if count != 2:
        return lax.all_gather(block, "tensor", axis=1, tiled=True)
    other = lax.ppermute(block, "tensor", [(0, 1), (1, 0)])
    first = jnp.where(rank == 0, block, other)
    second = jnp.where(rank == 0, other, block)
    return jnp.concatenate([first, second], axis=1)


def projected(query_states, doc_states, proj_weight, left_proj):
    count = lax.axis_size("tensor")
    rank = lax.axis_index("tensor")
    rows = query_states.shape[0]
    left_share = left_proj.shape[1] // count
    full = gather_columns(jnp.concatenate([query_states, doc_states], axis=0), count, rank)
    raw = jnp.dot(full, proj_weight, preferred_element_type=f32)
    left_mine = lax.dynamic_slice_in_dim(left_proj, rank * left_share, left_share, 1)
    left = jnp.dot(full, left_mine, preferred_element_type=f32)
    scale = lax.rsqrt(lax.psum(jnp.sum(raw * raw, axis=1), "tensor") + epsilon)
    unit = (raw * scale[:, None]).astype(bf16)
    return unit, scale, left


def local(query_states, doc_states, proj_weight, left_proj, right_proj, positives):
    count = lax.axis_size("tensor")
    rank = lax.axis_index("tensor")
    dp_count = lax.axis_size("dp")
    rows = query_states.shape[0]
    share = rows // count
    unit, scale, left = projected(query_states, doc_states, proj_weight, left_proj)
    doc_local = unit[rows:]
    if count == 2:
        mine = lax.dynamic_slice_in_dim(doc_local, rank * share, share, 0)
        theirs = lax.dynamic_slice_in_dim(doc_local, (1 - rank) * share, share, 0)
        came = lax.ppermute(theirs, "tensor", [(0, 1), (1, 0)])
        first = jnp.where(rank == 0, mine, came)
        second = jnp.where(rank == 0, came, mine)
        doc_mine = jnp.concatenate([first, second], axis=1)
    else:
        doc_mine = lax.all_to_all(doc_local, "tensor", split_axis=0, concat_axis=1, tiled=True)
    doc_block = lax.all_gather(doc_mine, "dp", axis=0, tiled=True)
    query_unit = gather_columns(unit[:rows], count, rank)
    top = jnp.concatenate([query_unit, right_proj.T], axis=0)
    product = lax.dot_general(top, doc_block, (((1,), (1,)), ((), ())), preferred_element_type=f32)
    scores = product[:rows] * inverse_temp
    doc_right = product[rows:] * inverse_temp
    query_right = jnp.dot(query_unit, right_proj, preferred_element_type=f32)
    top_part = jnp.max(scores, axis=1)
    sum_part = jnp.sum(jnp.exp(scores - top_part[:, None]), axis=1)
    parts = lax.all_gather(jnp.stack([top_part, sum_part]), "tensor")
    row_top = jnp.max(parts[:, 0], axis=0)
    lse = row_top + jnp.log(jnp.sum(parts[:, 1] * jnp.exp(parts[:, 0] - row_top), axis=0))
    column = jnp.arange(dp_count * share, dtype=jnp.int32)
    doc_ids = column // share * rows + rank * share + column % share
    onehot = (positives[:, None] == doc_ids[None, :]).astype(f32)
    weights = (jnp.exp(scores - lse[:, None]) - onehot).astype(bf16)
    weighted = weights.astype(f32) * scores
    query_sum = halves(
        lax.dot_general(
            weights, split_hi_lo(doc_right, 0), (((1,), (1,)), ((), ())), preferred_element_type=f32
        ),
        1,
    )
    query_part = query_sum - jnp.sum(weighted, axis=1)[:, None] * query_right
    doc_sum = halves(
        lax.dot_general(
            split_hi_lo(query_right * inverse_temp, 1), weights, (((0,), (0,)), ((), ())),
            preferred_element_type=f32,
        ),
        0,
    )
    doc_part = doc_sum - jnp.sum(weighted, axis=0)[None, :] * (doc_right * (1.0 / inverse_temp))
    blocks = doc_part.reshape(doc_part.shape[0], dp_count, share).transpose(1, 2, 0)
    came = lax.all_to_all(blocks, "dp", split_axis=0, concat_axis=0, tiled=True)
    right_mine = jnp.sum(came, axis=0)
    right_doc = lax.all_gather(right_mine, "tensor", axis=0, tiled=True) * scale[rows:, None]
    right_query = lax.psum(query_part, "tensor") * scale[:rows, None]
    return (outer_rows(left[:rows], right_query), outer_rows(left[rows:], right_doc))


MESH = pl.DeviceIdType.MESH


def dot_rows(a, b):
    return lax.dot_general(a, b, (((1,), (1,)), ((), ())), preferred_element_type=f32)


def dot_plain(a, b):
    return lax.dot_general(a, b, (((1,), (0,)), ((), ())), preferred_element_type=f32)


def dot_down(a, b):
    return lax.dot_general(a, b, (((0,), (0,)), ((), ())), preferred_element_type=f32)


def hi_lo(value):
    hi = value.astype(bf16)
    return hi, (value - hi.astype(f32)).astype(bf16)


pieces = 4
tiles = 4


def ring_kernel(
    dp_count, rows, share, width,
    query_ref, doc_ref, weight_ref, left_ref, right_ref, pos_ref,
    query_out, doc_out, scale_out, left_out,
    weight, query_raw, doc_raw, query_came, doc_came, top_ref,
    held, full, mine, in_buf, stat_out, stat_in, qr_out, qr_in, qrt_out, qrt_in,
    sum_out, sum_in, query_send, query_in, last_in,
    right_send, left_send, ring_recv, half_recv, sib_send, sib_recv, x_send, x_recv,
    all_send, all_recv, misc_send, misc_recv, local_sem, state_send, state_recv,
):
    depth = query_ref.shape[1]
    piece = depth // pieces
    tile = depth // tiles
    chips = dp_count // 2
    half = chips // 2
    me = lax.axis_index("dp")
    side = lax.axis_index("tensor")
    core = me % 2
    chip = me // 2
    spot = chip // 2 + (chip % 2) * (chips - 1 - 2 * (chip // 2))

    def dp_at(step, flag):
        q = (spot + step) % chips
        upper = q // half
        where = 2 * q + upper * (2 * (chips - 1 - q) + 1 - 2 * q)
        return 2 * where + core + flag * (1 - 2 * core)

    across = (me, 1 - side)
    right = (dp_at(1, 0), side)
    left = (dp_at(chips - 1, 0), side)
    sibling = (dp_at(0, 1), side)

    def send(src, dst, send_sem, recv_sem, device):
        return pltpu.make_async_remote_copy(
            src_ref=src, dst_ref=dst, send_sem=send_sem, recv_sem=recv_sem,
            device_id=device, device_id_type=MESH,
        )

    loads = [
        pltpu.make_async_copy(
            weight_ref.at[pl.ds(pl.multiple_of(which * depth, depth), depth)], weight.at[i], local_sem.at[i]
        )
        for i, which in enumerate((side, 1 - side))
    ]
    for load in loads:
        load.start()

    barrier = pltpu.get_barrier_semaphore()
    pl.semaphore_signal(barrier, inc=1, device_id=across, device_id_type=MESH)

    @pl.loop(1, dp_count)
    def _(b):
        pl.semaphore_signal(
            barrier, inc=1, device_id=(dp_at(b // 2, b % 2), side), device_id_type=MESH
        )

    pl.semaphore_wait(barrier, dp_count)

    def slot(r):
        return held.at[2 * (r % chips)]

    def to_right(s):
        if s < half:
            return send(slot(chips - s + 1), held.at[2 * (chips - s)], right_send.at[s],
                        ring_recv.at[chips - s], right)
        return send(slot(chips - s + 1).at[pl.ds(0, share)], held.at[2 * half, pl.ds(0, share)],
                    right_send.at[s], ring_recv.at[half], right)

    def to_left(s):
        if s < half:
            return send(slot(s - 1), held.at[2 * s], left_send.at[s], ring_recv.at[s], left)
        return send(slot(s - 1).at[pl.ds(share, share)], held.at[2 * half, pl.ds(share, share)],
                    left_send.at[s], half_recv, left)

    def to_sibling(r):
        return send(slot(r), held.at[2 * r + 1], sib_send.at[r], sib_recv.at[r], sibling)

    my_docs = pl.ds(pl.multiple_of(side * share, share), share)
    other_docs = pl.ds(pl.multiple_of((1 - side) * share, share), share)

    def swap(b):
        return send(full.at[b, other_docs], in_buf.at[b], x_send.at[b], x_recv.at[b], across)

    def score(r):
        both = held[pl.ds(2 * r, 2)].reshape(2 * rows, depth)
        full[pl.ds(2 * r, 2)] = dot_rows(both, top_ref[...]).reshape(2, rows, rows + width)
        swap(2 * r).start()
        swap(2 * r + 1).start()

    diagonal = lax.broadcasted_iota(jnp.int32, (rows, rows), 0) == lax.broadcasted_iota(
        jnp.int32, (rows, rows), 1
    )

    def as_row(col):
        return jnp.sum(jnp.where(diagonal, col, 0.0), axis=0, keepdims=True)

    def as_col(row):
        return jnp.sum(jnp.where(diagonal, row, 0.0), axis=1, keepdims=True)

    def swap_piece(src, dst, k, at):
        part = pl.ds(k * piece, piece)
        return send(src.at[:, part], dst.at[:, part], state_send.at[at + k], state_recv.at[at + k], across)

    doc_pieces = [swap_piece(doc_ref, doc_came, k, 0) for k in range(pieces)]
    query_pieces = [swap_piece(query_ref, query_came, k, pieces) for k in range(pieces)]
    for copy in doc_pieces:
        copy.start()

    def left_of(which):
        return left_ref[:, pl.ds(pl.multiple_of(which * depth, depth), depth)]

    def project_mine(states, raw):
        @pl.loop(0, tiles)
        def _(n):
            cols = pl.ds(pl.multiple_of(n * tile, tile), tile)
            raw[:, cols] = dot_plain(states[...], weight[0, :, cols])

    def project_piece(states, raw, k):
        part = pl.ds(k * piece, piece)

        @pl.loop(0, tiles)
        def _(n):
            cols = pl.ds(pl.multiple_of(n * tile, tile), tile)
            raw[:, cols] += dot_plain(states[:, part], weight[1, part, cols])

    def squares(raw):
        def add(n, total):
            block = raw[:, pl.ds(pl.multiple_of(n * 128, 128), 128)]
            return total + block * block

        total = lax.fori_loop(0, depth // 128, add, jnp.zeros((rows, 128), f32))
        return jnp.sum(total, axis=1, keepdims=True)

    def stat_copy(i):
        return send(stat_out.at[i], stat_in.at[i], misc_send.at[i], misc_recv.at[i], across)

    def normalize(raw, scale, store):
        @pl.loop(0, tiles)
        def _(n):
            cols = pl.ds(pl.multiple_of(n * tile, tile), tile)
            store(cols, (raw[:, cols] * scale).astype(bf16))

    def store_doc(cols, value):
        held[0, :, cols] = value

    def store_query(cols, value):
        top_ref[pl.ds(0, rows), cols] = value

    loads[0].wait()
    project_mine(doc_ref, doc_raw)
    project_mine(query_ref, query_raw)
    left_out[pl.ds(0, rows), :] = dot_rows(query_ref[...], left_of(side))
    left_out[pl.ds(rows, rows), :] = dot_rows(doc_ref[...], left_of(side))
    loads[1].wait()
    for k in range(pieces):
        doc_pieces[k].wait_recv()
        project_piece(doc_came, doc_raw, k)
    doc_sq = as_row(squares(doc_raw))
    stat_out[0] = jnp.broadcast_to(doc_sq, (8, rows))
    stat_copy(0).start()
    for copy in query_pieces:
        copy.start()
    left_out[pl.ds(rows, rows), :] += dot_rows(doc_came[...], left_of(1 - side))
    stat_copy(0).wait()
    doc_scale = lax.rsqrt(doc_sq + stat_in[0, pl.ds(0, 1), :] + epsilon)
    scale_out[...] = jnp.broadcast_to(doc_scale, (8, rows))
    normalize(doc_raw, as_col(doc_scale), store_doc)
    to_right(1).start()
    to_left(1).start()
    to_sibling(0).start()
    top_ref[pl.ds(rows, width), :] = right_ref[...]
    for k in range(pieces):
        query_pieces[k].wait_recv()
        project_piece(query_came, query_raw, k)
    query_sq = squares(query_raw)
    stat_out[1] = jnp.broadcast_to(as_row(query_sq), (8, rows))
    stat_copy(1).start()
    left_out[pl.ds(0, rows), :] += dot_rows(query_came[...], left_of(1 - side))
    stat_copy(1).wait()
    query_scale = lax.rsqrt(query_sq + as_col(stat_in[1, pl.ds(0, 1), :]) + epsilon)
    normalize(query_raw, query_scale, store_query)
    qr_swap = send(qr_out, qr_in, misc_send.at[3], misc_recv.at[3], across)
    qrt_swap = send(qrt_out, qrt_in, misc_send.at[4], misc_recv.at[4], across)
    for s in range(1, half):
        to_right(s).wait_recv()
        to_right(s + 1).start()
        to_sibling(chips - s).start()
        to_left(s).wait_recv()
        to_left(s + 1).start()
        to_sibling(s).start()
        if s == 1:
            qr_out[...] = dot_rows(top_ref[pl.ds(0, rows), :], top_ref[pl.ds(rows, width), :])
            qrt_out[...] = dot_rows(top_ref[pl.ds(rows, width), :], top_ref[pl.ds(0, rows), :])
            qr_swap.start()
            qrt_swap.start()
            to_sibling(0).wait_recv()

            score(0)

        to_sibling(chips - s).wait_recv()
        to_sibling(s).wait_recv()

        @pl.loop(0, 2)
        def _(k):
            score(s + k * (chips - 2 * s))

    to_right(half).wait_recv()
    to_left(half).wait_recv()
    to_sibling(half).start()
    to_sibling(half).wait_recv()
    score(half)
    for s in range(1, half + 1):
        to_right(s).wait_send()
        to_left(s).wait_send()
    for r in range(chips):
        to_sibling(r).wait_send()
    for copy in doc_pieces + query_pieces:
        copy.wait_send()

    def add_up(b, top):
        swap(b).wait()
        total = full[b, my_docs, :] + in_buf[b]
        mine[b] = total
        return jnp.maximum(top, total[:, :rows] * inverse_temp)

    top_wide = lax.fori_loop(0, dp_count, add_up, jnp.full((share, rows), -jnp.inf, f32))
    top_mine = jnp.max(top_wide, axis=0, keepdims=True)

    def add_exp(b, total):
        return total + jnp.exp(mine[b, :, pl.ds(0, rows)] * inverse_temp - top_mine)

    sum_wide = lax.fori_loop(0, dp_count, add_exp, jnp.zeros((share, rows), f32))
    sum_mine = jnp.sum(sum_wide, axis=0, keepdims=True)
    stat_out[2] = jnp.concatenate(
        [jnp.broadcast_to(top_mine, (4, rows)), jnp.broadcast_to(sum_mine, (4, rows))], axis=0
    )
    stat_copy(2).start()
    qr_swap.wait()
    qrt_swap.wait()
    query_turned = qrt_out[...] + qrt_in[...]
    right_hi, right_lo = hi_lo((qr_out[...] + qr_in[...]) * inverse_temp)
    stat_copy(2).wait()
    stats = stat_in[2]
    top_other = stats[0:1]
    sum_other = stats[4:5]
    row_top = jnp.maximum(top_mine, top_other)
    lse = row_top + jnp.log(
        sum_mine * jnp.exp(top_mine - row_top) + sum_other * jnp.exp(top_other - row_top)
    )
    positives = pos_ref[...]

    def share_out(b):
        return send(
            sum_out.at[b], sum_in.at[2 * ((chips - b // 2) % chips) + b % 2], all_send.at[b],
            all_recv.at[2 * ((chips - b // 2) % chips) + b % 2], (dp_at(b // 2, b % 2), side),
        )

    def gradients(b, carry):
        query_sum, inner_wide = carry
        scores = mine[b, :, pl.ds(0, rows)] * inverse_temp
        doc_right = mine[b][:, rows:]
        ids = lax.broadcasted_iota(jnp.int32, (share, rows), 0) + (
            dp_at(b // 2, b % 2) * rows + side * share
        )
        onehot = jnp.where(positives == ids, 1.0, 0.0)
        weights = (jnp.exp(scores - lse) - onehot).astype(bf16)
        weighted = weights.astype(f32) * scores
        doc_hi, doc_lo = hi_lo(doc_right * inverse_temp)
        query_sum = query_sum + dot_down(doc_hi, weights) + dot_down(doc_lo, weights)
        doc_sum = (
            dot_plain(weights, right_hi) + dot_plain(weights, right_lo)
            - jnp.sum(weighted, axis=1, keepdims=True) * doc_right
        )
        sum_out[b] = jnp.concatenate([doc_sum[: share // 2], doc_sum[share // 2 :]], axis=1)
        return query_sum, inner_wide + weighted

    carry = (jnp.zeros((width, rows), f32), jnp.zeros((share, rows), f32))

    def step(b, carry):
        carry = gradients(b, carry)
        share_out(b).start()
        return carry

    carry = lax.fori_loop(1, dp_count, step, carry)
    query_sum, inner_wide = gradients(0, carry)
    query_send[...] = query_sum - jnp.sum(inner_wide, axis=0, keepdims=True) * query_turned
    query_swap = send(query_send, query_in, misc_send.at[5], misc_recv.at[5], across)
    query_swap.start()

    @pl.loop(1, dp_count)
    def _(b):
        share_out(b).wait()

    def collect(b, total):
        return total + sum_in[b]

    doc_sum = lax.fori_loop(1, dp_count, collect, sum_out[0])
    doc_out[side] = doc_sum
    last_swap = send(doc_out.at[side], last_in, misc_send.at[6], misc_recv.at[6], across)
    last_swap.start()
    query_swap.wait()
    query_out[...] = (query_send[...] + query_in[...]) * as_row(query_scale)
    last_swap.wait()
    doc_out[1 - side] = last_in[...]


def ring_gradients(query_states, doc_states, proj_weight, left_turned, right_turned, positives, dp_count):
    chips = dp_count // 2
    rows, depth = doc_states.shape
    share = rows // 2
    width = right_turned.shape[0]
    dma = pltpu.SemaphoreType.DMA
    sums = pltpu.VMEM((dp_count, share // 2, 2 * width), f32)
    parts = pltpu.VMEM((dp_count, share, rows + width), f32)
    vmem = pl.BlockSpec(memory_space=pltpu.VMEM)
    raw = pltpu.VMEM((rows, depth), f32)
    states = pltpu.VMEM((rows, depth), bf16)
    return pl.pallas_call(
        functools.partial(ring_kernel, dp_count, rows, share, width),
        out_shape=(
            jax.ShapeDtypeStruct((width, rows), f32),
            jax.ShapeDtypeStruct((2, share // 2, 2 * width), f32),
            jax.ShapeDtypeStruct((8, rows), f32),
            jax.ShapeDtypeStruct((2 * rows, left_turned.shape[0]), f32),
        ),
        in_specs=[vmem, vmem, pl.BlockSpec(memory_space=pl.ANY), vmem, vmem, vmem],
        out_specs=(vmem, vmem, vmem, vmem),
        scratch_shapes=[
            pltpu.VMEM((2, depth, depth), bf16),
            raw, raw, states, states,
            pltpu.VMEM((rows + width, depth), bf16),
            pltpu.VMEM((dp_count, rows, depth), bf16),
            pltpu.VMEM((dp_count, rows, rows + width), f32), parts, parts,
            pltpu.VMEM((3, 8, rows), f32), pltpu.VMEM((3, 8, rows), f32),
            pltpu.VMEM((rows, width), f32), pltpu.VMEM((rows, width), f32),
            pltpu.VMEM((width, rows), f32), pltpu.VMEM((width, rows), f32),
            sums, sums,
            pltpu.VMEM((width, rows), f32), pltpu.VMEM((width, rows), f32),
            pltpu.VMEM((share // 2, 2 * width), f32),
            dma((chips,)), dma((chips,)), dma((chips,)), dma, dma((chips,)), dma((chips,)),
            dma((dp_count,)), dma((dp_count,)), dma((dp_count,)), dma((dp_count,)),
            dma((7,)), dma((7,)), dma((2,)), dma((2 * pieces,)), dma((2 * pieces,)),
        ],
        compiler_params=pltpu.CompilerParams(
            collective_id=0, has_side_effects=True, vmem_limit_bytes=57 * 2**20
        ),
    )(query_states, doc_states, proj_weight, left_turned, right_turned, positives)


def local_ring(query_states, doc_states, proj_weight, left_proj, right_proj, positives):
    rank = lax.axis_index("tensor")
    rows = query_states.shape[0]
    depth = proj_weight.shape[1]
    left_share = left_proj.shape[1] // 2
    right_mine = lax.dynamic_slice_in_dim(right_proj, rank * depth, depth, 0)
    left_mine = lax.dynamic_slice_in_dim(left_proj, rank * left_share, left_share, 1)
    right_query, right_doc, scale, left = ring_gradients(
        query_states, doc_states, proj_weight, left_mine.T, right_mine.T, positives[None, :],
        lax.axis_size("dp"),
    )
    right_doc = jnp.stack(jnp.split(right_doc, 2, axis=2), axis=1).reshape(rows, -1) * scale[0][:, None]
    return (outer_rows(left[:rows], right_query.T), outer_rows(left[rows:], right_doc))


def solution(mesh):
    ring = mesh.shape["tensor"] == 2 and mesh.shape["dp"] % 4 == 0 and mesh.shape["dp"] >= 8
    placed = (P("dp", "tensor"), P("dp", "tensor"), P(None, "tensor"), P(), P(), P("dp"))
    return jax.shard_map(
        local_ring if ring else local,
        mesh=mesh,
        in_specs=placed,
        out_specs=(P("dp", "tensor"), P("dp", "tensor")),
        check_vma=False,
    )
```

```python
import functools

import jax
import jax.numpy as jnp
from jax import lax
from jax.experimental import pallas as pl
from jax.experimental.pallas import tpu as pltpu
from jax.sharding import PartitionSpec as P

epsilon = 1e-06
inverse_temp = 100.0
f32 = jnp.float32
bf16 = jnp.bfloat16


def outer_rows(left_side, right_side):
    return (left_side[:, :, None] * right_side[:, None, :]).reshape(left_side.shape[0], -1)


def split_hi_lo(value, axis):
    hi = value.astype(bf16)
    lo = (value - hi.astype(f32)).astype(bf16)
    return jnp.concatenate([hi, lo], axis=axis)


def halves(product, axis):
    size = product.shape[axis] // 2
    return lax.slice_in_dim(product, 0, size, axis=axis) + lax.slice_in_dim(product, size, 2 * size, axis=axis)


def gather_columns(block, count, rank):
    if count != 2:
        return lax.all_gather(block, "tensor", axis=1, tiled=True)
    other = lax.ppermute(block, "tensor", [(0, 1), (1, 0)])
    first = jnp.where(rank == 0, block, other)
    second = jnp.where(rank == 0, other, block)
    return jnp.concatenate([first, second], axis=1)


def projected(query_states, doc_states, proj_weight, left_proj):
    count = lax.axis_size("tensor")
    rank = lax.axis_index("tensor")
    rows = query_states.shape[0]
    left_share = left_proj.shape[1] // count
    full = gather_columns(jnp.concatenate([query_states, doc_states], axis=0), count, rank)
    raw = jnp.dot(full, proj_weight, preferred_element_type=f32)
    left_mine = lax.dynamic_slice_in_dim(left_proj, rank * left_share, left_share, 1)
    left = jnp.dot(full, left_mine, preferred_element_type=f32)
    scale = lax.rsqrt(lax.psum(jnp.sum(raw * raw, axis=1), "tensor") + epsilon)
    unit = (raw * scale[:, None]).astype(bf16)
    return unit, scale, left


def local(query_states, doc_states, proj_weight, left_proj, right_proj, positives):
    count = lax.axis_size("tensor")
    rank = lax.axis_index("tensor")
    dp_count = lax.axis_size("dp")
    rows = query_states.shape[0]
    share = rows // count
    unit, scale, left = projected(query_states, doc_states, proj_weight, left_proj)
    doc_local = unit[rows:]
    if count == 2:
        mine = lax.dynamic_slice_in_dim(doc_local, rank * share, share, 0)
        theirs = lax.dynamic_slice_in_dim(doc_local, (1 - rank) * share, share, 0)
        came = lax.ppermute(theirs, "tensor", [(0, 1), (1, 0)])
        first = jnp.where(rank == 0, mine, came)
        second = jnp.where(rank == 0, came, mine)
        doc_mine = jnp.concatenate([first, second], axis=1)
    else:
        doc_mine = lax.all_to_all(doc_local, "tensor", split_axis=0, concat_axis=1, tiled=True)
    doc_block = lax.all_gather(doc_mine, "dp", axis=0, tiled=True)
    query_unit = gather_columns(unit[:rows], count, rank)
    top = jnp.concatenate([query_unit, right_proj.T], axis=0)
    product = lax.dot_general(top, doc_block, (((1,), (1,)), ((), ())), preferred_element_type=f32)
    scores = product[:rows] * inverse_temp
    doc_right = product[rows:] * inverse_temp
    query_right = jnp.dot(query_unit, right_proj, preferred_element_type=f32)
    top_part = jnp.max(scores, axis=1)
    sum_part = jnp.sum(jnp.exp(scores - top_part[:, None]), axis=1)
    parts = lax.all_gather(jnp.stack([top_part, sum_part]), "tensor")
    row_top = jnp.max(parts[:, 0], axis=0)
    lse = row_top + jnp.log(jnp.sum(parts[:, 1] * jnp.exp(parts[:, 0] - row_top), axis=0))
    column = jnp.arange(dp_count * share, dtype=jnp.int32)
    doc_ids = column // share * rows + rank * share + column % share
    onehot = (positives[:, None] == doc_ids[None, :]).astype(f32)
    weights = (jnp.exp(scores - lse[:, None]) - onehot).astype(bf16)
    weighted = weights.astype(f32) * scores
    query_sum = halves(
        lax.dot_general(
            weights, split_hi_lo(doc_right, 0), (((1,), (1,)), ((), ())), preferred_element_type=f32
        ),
        1,
    )
    query_part = query_sum - jnp.sum(weighted, axis=1)[:, None] * query_right
    doc_sum = halves(
        lax.dot_general(
            split_hi_lo(query_right * inverse_temp, 1), weights, (((0,), (0,)), ((), ())),
            preferred_element_type=f32,
        ),
        0,
    )
    doc_part = doc_sum - jnp.sum(weighted, axis=0)[None, :] * (doc_right * (1.0 / inverse_temp))
    blocks = doc_part.reshape(doc_part.shape[0], dp_count, share).transpose(1, 2, 0)
    came = lax.all_to_all(blocks, "dp", split_axis=0, concat_axis=0, tiled=True)
    right_mine = jnp.sum(came, axis=0)
    right_doc = lax.all_gather(right_mine, "tensor", axis=0, tiled=True) * scale[rows:, None]
    right_query = lax.psum(query_part, "tensor") * scale[:rows, None]
    return (outer_rows(left[:rows], right_query), outer_rows(left[rows:], right_doc))


MESH = pl.DeviceIdType.MESH


def dot_rows(a, b):
    return lax.dot_general(a, b, (((1,), (1,)), ((), ())), preferred_element_type=f32)


def dot_plain(a, b):
    return lax.dot_general(a, b, (((1,), (0,)), ((), ())), preferred_element_type=f32)


def dot_down(a, b):
    return lax.dot_general(a, b, (((0,), (0,)), ((), ())), preferred_element_type=f32)


def hi_lo(value):
    hi = value.astype(bf16)
    return hi, (value - hi.astype(f32)).astype(bf16)


pieces = 4
tiles = 4


def ring_kernel(
    dp_count, rows, share, width,
    query_ref, doc_ref, weight_ref, left_ref, right_ref, pos_ref,
    query_out, doc_out, scale_out, left_out,
    weight, query_raw, doc_raw, query_came, doc_came, top_ref,
    held, full, mine, in_buf, stat_out, stat_in, qr_out, qr_in, qrt_out, qrt_in,
    sum_out, sum_in, query_send, query_in, last_in,
    right_send, left_send, ring_recv, half_recv, sib_send, sib_recv, x_send, x_recv,
    all_send, all_recv, misc_send, misc_recv, local_sem, state_send, state_recv,
):
    depth = query_ref.shape[1]
    piece = depth // pieces
    tile = depth // tiles
    chips = dp_count // 2
    half = chips // 2
    me = lax.axis_index("dp")
    side = lax.axis_index("tensor")
    core = me % 2
    chip = me // 2
    spot = chip // 2 + (chip % 2) * (chips - 1 - 2 * (chip // 2))

    def dp_at(step, flag):
        q = (spot + step) % chips
        upper = q // half
        where = 2 * q + upper * (2 * (chips - 1 - q) + 1 - 2 * q)
        return 2 * where + core + flag * (1 - 2 * core)

    across = (me, 1 - side)
    right = (dp_at(1, 0), side)
    left = (dp_at(chips - 1, 0), side)
    sibling = (dp_at(0, 1), side)

    def send(src, dst, send_sem, recv_sem, device):
        return pltpu.make_async_remote_copy(
            src_ref=src, dst_ref=dst, send_sem=send_sem, recv_sem=recv_sem,
            device_id=device, device_id_type=MESH,
        )

    loads = [
        pltpu.make_async_copy(
            weight_ref.at[pl.ds(pl.multiple_of(which * depth, depth), depth)], weight.at[i], local_sem.at[i]
        )
        for i, which in enumerate((side, 1 - side))
    ]
    for load in loads:
        load.start()

    barrier = pltpu.get_barrier_semaphore()
    pl.semaphore_signal(barrier, inc=1, device_id=across, device_id_type=MESH)

    @pl.loop(1, dp_count)
    def _(b):
        pl.semaphore_signal(
            barrier, inc=1, device_id=(dp_at(b // 2, b % 2), side), device_id_type=MESH
        )

    pl.semaphore_wait(barrier, dp_count)

    def slot(r):
        return held.at[2 * (r % chips)]

    def to_right(s):
        if s < half:
            return send(slot(chips - s + 1), held.at[2 * (chips - s)], right_send.at[s],
                        ring_recv.at[chips - s], right)
        return send(slot(chips - s + 1).at[pl.ds(0, share)], held.at[2 * half, pl.ds(0, share)],
                    right_send.at[s], ring_recv.at[half], right)

    def to_left(s):
        if s < half:
            return send(slot(s - 1), held.at[2 * s], left_send.at[s], ring_recv.at[s], left)
        return send(slot(s - 1).at[pl.ds(share, share)], held.at[2 * half, pl.ds(share, share)],
                    left_send.at[s], half_recv, left)

    def to_sibling(r):
        return send(slot(r), held.at[2 * r + 1], sib_send.at[r], sib_recv.at[r], sibling)

    my_docs = pl.ds(pl.multiple_of(side * share, share), share)
    other_docs = pl.ds(pl.multiple_of((1 - side) * share, share), share)

    def swap(b):
        return send(full.at[b, other_docs], in_buf.at[b], x_send.at[b], x_recv.at[b], across)

    def score(r):
        both = held[pl.ds(2 * r, 2)].reshape(2 * rows, depth)
        full[pl.ds(2 * r, 2)] = dot_rows(both, top_ref[...]).reshape(2, rows, rows + width)
        swap(2 * r).start()
        swap(2 * r + 1).start()

    diagonal = lax.broadcasted_iota(jnp.int32, (rows, rows), 0) == lax.broadcasted_iota(
        jnp.int32, (rows, rows), 1
    )

    def as_row(col):
        return jnp.sum(jnp.where(diagonal, col, 0.0), axis=0, keepdims=True)

    def as_col(row):
        return jnp.sum(jnp.where(diagonal, row, 0.0), axis=1, keepdims=True)

    def swap_piece(src, dst, k, at):
        part = pl.ds(k * piece, piece)
        return send(src.at[:, part], dst.at[:, part], state_send.at[at + k], state_recv.at[at + k], across)

    doc_pieces = [swap_piece(doc_ref, doc_came, k, 0) for k in range(pieces)]
    query_pieces = [swap_piece(query_ref, query_came, k, pieces) for k in range(pieces)]
    for copy in doc_pieces:
        copy.start()

    def left_of(which):
        return left_ref[:, pl.ds(pl.multiple_of(which * depth, depth), depth)]

    def project_mine(states, raw):
        @pl.loop(0, tiles)
        def _(n):
            cols = pl.ds(pl.multiple_of(n * tile, tile), tile)
            raw[:, cols] = dot_plain(states[...], weight[0, :, cols])

    def project_piece(states, raw, k):
        part = pl.ds(k * piece, piece)

        @pl.loop(0, tiles)
        def _(n):
            cols = pl.ds(pl.multiple_of(n * tile, tile), tile)
            raw[:, cols] += dot_plain(states[:, part], weight[1, part, cols])

    def squares(raw):
        def add(n, total):
            block = raw[:, pl.ds(pl.multiple_of(n * 128, 128), 128)]
            return total + block * block

        total = lax.fori_loop(0, depth // 128, add, jnp.zeros((rows, 128), f32))
        return jnp.sum(total, axis=1, keepdims=True)

    def stat_copy(i):
        return send(stat_out.at[i], stat_in.at[i], misc_send.at[i], misc_recv.at[i], across)

    def normalize(raw, scale, store):
        @pl.loop(0, tiles)
        def _(n):
            cols = pl.ds(pl.multiple_of(n * tile, tile), tile)
            store(cols, (raw[:, cols] * scale).astype(bf16))

    def store_doc(cols, value):
        held[0, :, cols] = value

    def store_query(cols, value):
        top_ref[pl.ds(0, rows), cols] = value

    def pass_on(s):
        to_right(s).wait_recv()
        to_right(s + 1).start()
        to_sibling(chips - s).start()
        to_left(s).wait_recv()
        to_left(s + 1).start()
        to_sibling(s).start()

    loads[0].wait()
    project_mine(doc_ref, doc_raw)
    project_mine(query_ref, query_raw)
    left_out[pl.ds(0, rows), :] = dot_rows(query_ref[...], left_of(side))
    left_out[pl.ds(rows, rows), :] = dot_rows(doc_ref[...], left_of(side))
    loads[1].wait()
    for k in range(pieces):
        doc_pieces[k].wait_recv()
        project_piece(doc_came, doc_raw, k)
    doc_sq = as_row(squares(doc_raw))
    stat_out[0] = jnp.broadcast_to(doc_sq, (8, rows))
    stat_copy(0).start()
    for copy in query_pieces:
        copy.start()
    left_out[pl.ds(rows, rows), :] += dot_rows(doc_came[...], left_of(1 - side))
    stat_copy(0).wait()
    doc_scale = lax.rsqrt(doc_sq + stat_in[0, pl.ds(0, 1), :] + epsilon)
    scale_out[...] = jnp.broadcast_to(doc_scale, (8, rows))
    normalize(doc_raw, as_col(doc_scale), store_doc)
    to_right(1).start()
    to_left(1).start()
    to_sibling(0).start()
    top_ref[pl.ds(rows, width), :] = right_ref[...]
    for k in range(pieces):
        query_pieces[k].wait_recv()
        project_piece(query_came, query_raw, k)
    query_sq = squares(query_raw)
    stat_out[1] = jnp.broadcast_to(as_row(query_sq), (8, rows))
    stat_copy(1).start()
    left_out[pl.ds(0, rows), :] += dot_rows(query_came[...], left_of(1 - side))
    pass_on(1)
    stat_copy(1).wait()
    query_scale = lax.rsqrt(query_sq + as_col(stat_in[1, pl.ds(0, 1), :]) + epsilon)
    normalize(query_raw, query_scale, store_query)
    qr_swap = send(qr_out, qr_in, misc_send.at[3], misc_recv.at[3], across)
    qrt_swap = send(qrt_out, qrt_in, misc_send.at[4], misc_recv.at[4], across)
    for s in range(1, half):
        if s > 1:
            pass_on(s)
        if s == 1:
            qr_out[...] = dot_rows(top_ref[pl.ds(0, rows), :], top_ref[pl.ds(rows, width), :])
            qrt_out[...] = dot_rows(top_ref[pl.ds(rows, width), :], top_ref[pl.ds(0, rows), :])
            qr_swap.start()
            qrt_swap.start()
            to_sibling(0).wait_recv()

            score(0)

        to_sibling(chips - s).wait_recv()
        to_sibling(s).wait_recv()

        @pl.loop(0, 2)
        def _(k):
            score(s + k * (chips - 2 * s))

    def add_up(b, top):
        swap(b).wait()
        total = full[b, my_docs, :] + in_buf[b]
        mine[b] = total
        return jnp.maximum(top, total[:, :rows] * inverse_temp)

    top_wide = jnp.full((share, rows), -jnp.inf, f32)
    top_wide = lax.fori_loop(0, 2 * half - 2, add_up, top_wide)
    top_wide = lax.fori_loop(2 * half + 4, dp_count, add_up, top_wide)
    to_right(half).wait_recv()
    to_left(half).wait_recv()
    to_sibling(half).start()
    to_sibling(half).wait_recv()
    score(half)
    for s in range(1, half + 1):
        to_right(s).wait_send()
        to_left(s).wait_send()
    for r in range(chips):
        to_sibling(r).wait_send()
    for copy in doc_pieces + query_pieces:
        copy.wait_send()

    top_wide = lax.fori_loop(2 * half - 2, 2 * half + 4, add_up, top_wide)
    top_mine = jnp.max(top_wide, axis=0, keepdims=True)

    def add_exp(b, total):
        return total + jnp.exp(mine[b, :, pl.ds(0, rows)] * inverse_temp - top_mine)

    sum_wide = lax.fori_loop(0, dp_count, add_exp, jnp.zeros((share, rows), f32))
    sum_mine = jnp.sum(sum_wide, axis=0, keepdims=True)
    stat_out[2] = jnp.concatenate(
        [jnp.broadcast_to(top_mine, (4, rows)), jnp.broadcast_to(sum_mine, (4, rows))], axis=0
    )
    stat_copy(2).start()
    qr_swap.wait()
    qrt_swap.wait()
    query_turned = qrt_out[...] + qrt_in[...]
    right_hi, right_lo = hi_lo((qr_out[...] + qr_in[...]) * inverse_temp)
    stat_copy(2).wait()
    stats = stat_in[2]
    top_other = stats[0:1]
    sum_other = stats[4:5]
    row_top = jnp.maximum(top_mine, top_other)
    lse = row_top + jnp.log(
        sum_mine * jnp.exp(top_mine - row_top) + sum_other * jnp.exp(top_other - row_top)
    )
    positives = pos_ref[...]

    def share_out(b):
        return send(
            sum_out.at[b], sum_in.at[2 * ((chips - b // 2) % chips) + b % 2], all_send.at[b],
            all_recv.at[2 * ((chips - b // 2) % chips) + b % 2], (dp_at(b // 2, b % 2), side),
        )

    def gradients(b, carry):
        query_sum, inner_wide = carry
        scores = mine[b, :, pl.ds(0, rows)] * inverse_temp
        doc_right = mine[b][:, rows:]
        ids = lax.broadcasted_iota(jnp.int32, (share, rows), 0) + (
            dp_at(b // 2, b % 2) * rows + side * share
        )
        onehot = jnp.where(positives == ids, 1.0, 0.0)
        weights = (jnp.exp(scores - lse) - onehot).astype(bf16)
        weighted = weights.astype(f32) * scores
        doc_hi, doc_lo = hi_lo(doc_right * inverse_temp)
        query_sum = query_sum + dot_down(doc_hi, weights) + dot_down(doc_lo, weights)
        doc_sum = (
            dot_plain(weights, right_hi) + dot_plain(weights, right_lo)
            - jnp.sum(weighted, axis=1, keepdims=True) * doc_right
        )
        sum_out[b] = jnp.concatenate([doc_sum[: share // 2], doc_sum[share // 2 :]], axis=1)
        return query_sum, inner_wide + weighted

    carry = (jnp.zeros((width, rows), f32), jnp.zeros((share, rows), f32))

    def step(b, carry):
        carry = gradients(b, carry)
        share_out(b).start()
        return carry

    carry = lax.fori_loop(1, dp_count, step, carry)
    query_sum, inner_wide = gradients(0, carry)
    query_send[...] = query_sum - jnp.sum(inner_wide, axis=0, keepdims=True) * query_turned
    query_swap = send(query_send, query_in, misc_send.at[5], misc_recv.at[5], across)
    query_swap.start()

    @pl.loop(1, dp_count)
    def _(b):
        share_out(b).wait()

    def collect(b, total):
        return total + sum_in[b]

    doc_sum = lax.fori_loop(1, dp_count, collect, sum_out[0])
    doc_out[side] = doc_sum
    last_swap = send(doc_out.at[side], last_in, misc_send.at[6], misc_recv.at[6], across)
    last_swap.start()
    query_swap.wait()
    query_out[...] = (query_send[...] + query_in[...]) * as_row(query_scale)
    last_swap.wait()
    doc_out[1 - side] = last_in[...]


def ring_gradients(query_states, doc_states, proj_weight, left_turned, right_turned, positives, dp_count):
    chips = dp_count // 2
    rows, depth = doc_states.shape
    share = rows // 2
    width = right_turned.shape[0]
    dma = pltpu.SemaphoreType.DMA
    sums = pltpu.VMEM((dp_count, share // 2, 2 * width), f32)
    parts = pltpu.VMEM((dp_count, share, rows + width), f32)
    vmem = pl.BlockSpec(memory_space=pltpu.VMEM)
    raw = pltpu.VMEM((rows, depth), f32)
    states = pltpu.VMEM((rows, depth), bf16)
    return pl.pallas_call(
        functools.partial(ring_kernel, dp_count, rows, share, width),
        out_shape=(
            jax.ShapeDtypeStruct((width, rows), f32),
            jax.ShapeDtypeStruct((2, share // 2, 2 * width), f32),
            jax.ShapeDtypeStruct((8, rows), f32),
            jax.ShapeDtypeStruct((2 * rows, left_turned.shape[0]), f32),
        ),
        in_specs=[vmem, vmem, pl.BlockSpec(memory_space=pl.ANY), vmem, vmem, vmem],
        out_specs=(vmem, vmem, vmem, vmem),
        scratch_shapes=[
            pltpu.VMEM((2, depth, depth), bf16),
            raw, raw, states, states,
            pltpu.VMEM((rows + width, depth), bf16),
            pltpu.VMEM((dp_count, rows, depth), bf16),
            pltpu.VMEM((dp_count, rows, rows + width), f32), parts, parts,
            pltpu.VMEM((3, 8, rows), f32), pltpu.VMEM((3, 8, rows), f32),
            pltpu.VMEM((rows, width), f32), pltpu.VMEM((rows, width), f32),
            pltpu.VMEM((width, rows), f32), pltpu.VMEM((width, rows), f32),
            sums, sums,
            pltpu.VMEM((width, rows), f32), pltpu.VMEM((width, rows), f32),
            pltpu.VMEM((share // 2, 2 * width), f32),
            dma((chips,)), dma((chips,)), dma((chips,)), dma, dma((chips,)), dma((chips,)),
            dma((dp_count,)), dma((dp_count,)), dma((dp_count,)), dma((dp_count,)),
            dma((7,)), dma((7,)), dma((2,)), dma((2 * pieces,)), dma((2 * pieces,)),
        ],
        compiler_params=pltpu.CompilerParams(
            collective_id=0, has_side_effects=True, vmem_limit_bytes=57 * 2**20
        ),
    )(query_states, doc_states, proj_weight, left_turned, right_turned, positives)


def local_ring(query_states, doc_states, proj_weight, left_proj, right_proj, positives):
    rank = lax.axis_index("tensor")
    rows = query_states.shape[0]
    depth = proj_weight.shape[1]
    left_share = left_proj.shape[1] // 2
    right_mine = lax.dynamic_slice_in_dim(right_proj, rank * depth, depth, 0)
    left_mine = lax.dynamic_slice_in_dim(left_proj, rank * left_share, left_share, 1)
    right_query, right_doc, scale, left = ring_gradients(
        query_states, doc_states, proj_weight, left_mine.T, right_mine.T, positives[None, :],
        lax.axis_size("dp"),
    )
    right_doc = jnp.stack(jnp.split(right_doc, 2, axis=2), axis=1).reshape(rows, -1) * scale[0][:, None]
    return (outer_rows(left[:rows], right_query.T), outer_rows(left[rows:], right_doc))


def solution(mesh):
    ring = mesh.shape["tensor"] == 2 and mesh.shape["dp"] % 4 == 0 and mesh.shape["dp"] >= 8
    placed = (P("dp", "tensor"), P("dp", "tensor"), P(None, "tensor"), P(), P(), P("dp"))
    return jax.shard_map(
        local_ring if ring else local,
        mesh=mesh,
        in_specs=placed,
        out_specs=(P("dp", "tensor"), P("dp", "tensor")),
        check_vma=False,
    )
```
